256 devices in a mesh: peer: 16 (over z_hi, x), fsdp: 16 (over y, z_lo, core).
Axes of the slice: x: 4, y: 4, z: 8 (z_hi: 4, z_lo: 2; z = z_hi * 2 + z_lo), core: 2. Of those that a mesh axis runs over, the one named last changes fastest.
Arguments:
- tokens: bfloat16 [65536, 4608], P(('peer', 'fsdp')), may hold values from -6 to 6
- cotangent: bfloat16 [65536, 1024], P(('peer', 'fsdp')), may hold values from -6 to 6
- weight: float32 [16, 4608, 1024], P('peer', 'fsdp'), may hold values from -4 to 4
- first_moment: float32 [16, 4608, 1024], P('peer', 'fsdp'), may hold values from -3 to 3
- second_moment: float32 [16, 4608, 1024], P('peer', 'fsdp'), may hold values from 0.25 to 4
- step: int32 [1], replicated, may hold values from 0 to 2999
Outputs:
- values: bfloat16 [65536, 1024], P(('peer', 'fsdp'))
- new_weight: float32 [16, 4608, 1024], P('peer', 'fsdp')
- new_first: float32 [16, 4608, 1024], P('peer', 'fsdp')
- new_second: float32 [16, 4608, 1024], P('peer', 'fsdp')
The draws below stay inside these ranges and needn't reach their ends.
All inputs are finite; a program needn't handle non-finite values.
Results may differ from the reference program's by a relative error of at most 0.0057.
Values may be sent and summed in bfloat16 or wider, within the bound.
No kernel may reach another device: no remote copies, remote signals or barrier semaphores. Data moves between devices by JAX's collectives and lax.ppermute only.
A program may use at most 128 MiB of HBM per device.

```python
import math
import jax
import jax.numpy as jnp
from jax import lax

D = 4608
KV = 1024
TOKENS = 65536
N_PEER = 16


def level_of(stream_key, dims, pieces, smallest, largest):
    gain = 1.0
    for dim, parts in pieces:
        steps = jax.random.uniform(jax.random.fold_in(jax.random.fold_in(stream_key, 6), dim), (parts,), jnp.float32, smallest / len(pieces), largest / len(pieces))
        gain = gain * jnp.repeat(jnp.exp(steps), dims[dim] // parts).reshape((-1,) + (1,) * (len(dims) - 1 - dim))
    return gain


def gaussian(rng, extent, deviation, most, shards=(), kind=jnp.bfloat16):
    level = level_of(rng, extent, shards, -0.22, 0.18) if shards else 1.0
    entries = jax.random.normal(rng, extent, jnp.float32) * deviation * level
    return jnp.minimum(jnp.maximum(entries, -most), most).astype(kind)


def setup_inputs(seed: int = 0) -> dict:
    keys = jax.random.split(jax.random.key(seed), 7)
    return {
        "tokens": gaussian(keys[0], (TOKENS, D), 1.0, 6.0, ((0, 256),)),
        "cotangent": gaussian(keys[1], (TOKENS, KV), 1.0, 6.0, ((0, 256),)),
        "weight": gaussian(keys[2], (N_PEER, D, KV), 1.0, 4.0, ((0, 16), (1, 16)), jnp.float32),
        "first_moment": gaussian(keys[3], (N_PEER, D, KV), 0.5, 3.0, ((0, 16), (1, 16)), jnp.float32),
        "second_moment": jnp.clip(jnp.exp(math.log(4.0) - 2.7725887 * jax.random.uniform(keys[4], (N_PEER, D, KV), jnp.float32) ** level_of(keys[4], (N_PEER, D, KV), ((0, 16), (1, 16)), -0.2, 0.2)), 0.25, 4.0),
        "step": jax.random.randint(keys[5], (1,), 0, 3000).astype(jnp.int32),
    }


def group_update(pack):
    rows, grads_out, master, first, second, count = pack
    widened = rows.astype(jnp.float32)
    normed = (widened * lax.rsqrt(lax.optimization_barrier(jnp.mean(widened * widened, axis=1, keepdims=True)) + 1e-06)).astype(jnp.bfloat16)
    factor = D ** (-0.5)
    wire_weight = master.astype(jnp.bfloat16)
    values = (jnp.dot(normed, wire_weight, preferred_element_type=jnp.float32) * factor).astype(jnp.bfloat16)
    grad = lax.dot_general(normed, grads_out, (((0,), (0,)), ((), ())), preferred_element_type=jnp.float32) * factor
    new_first = 0.9 * first + 0.1 * grad
    new_second = 0.999 * second + 0.001 * grad * grad
    corr_one = 1.0 - jnp.exp(count * jnp.log(jnp.float32(0.9)))
    corr_two = 1.0 - jnp.exp(count * jnp.log(jnp.float32(0.999)))
    change = new_first / corr_one / (jnp.sqrt(new_second / corr_two) + 1e-08)
    updated = master - 0.02 * (change + 0.1 * master)
    return (values, updated, new_first, new_second)

def reference(tokens, cotangent, weight, first_moment, second_moment, step):
    groups = weight.shape[0]
    levels = groups.bit_length() - 1
    rows = tokens.reshape(groups, -1, tokens.shape[1])
    grads_out = cotangent.reshape(groups, -1, cotangent.shape[1])
    count = (step[0] + 1).astype(jnp.float32) * jnp.ones((groups,), jnp.float32)
    values, updated, new_first, new_second = lax.map(group_update, (rows, grads_out, weight, first_moment, second_moment, count))
    shift_bit = jnp.left_shift(jnp.int32(1), (step[0] % levels).astype(jnp.int32))
    partner = jnp.bitwise_xor(jnp.arange(groups, dtype=jnp.int32), shift_bit)
    new_weight = 0.5 * (updated + updated[partner])
    return (values.reshape(-1, values.shape[2]), new_weight, new_first, new_second)
```

```python
from functools import partial

import jax
import jax.numpy as jnp
from jax import lax
from jax.sharding import PartitionSpec as P

D = 4608
Y, Z, C = 4, 2, 2
BF, F32 = jnp.bfloat16, jnp.float32


def hop(value, dy=0, dz=0, dc=0):
    pairs = []
    for i in range(Y * Z * C):
        y, z, c = i // (Z * C), i // C % Z, i % C
        pairs.append((i, ((y + dy) % Y * Z + (z ^ dz)) * C + (c ^ dc)))
    return lax.ppermute(value, "fsdp", pairs)


def gossip(value, bit):
    mask = 2**bit
    pairs = [(source, source ^ mask) for source in range(lax.axis_size("peer"))]
    return lax.ppermute(value, "peer", pairs)


def ordered(bit, mine, other, axis=0):
    first = jnp.where(bit == 0, mine, other)
    second = jnp.where(bit == 0, other, mine)
    return jnp.concatenate([first, second], axis=axis)


def rows_of(value, start, size):
    return lax.dynamic_slice_in_dim(value, start, size, 0)


def on_device(tokens, cotangent, weight, first_moment, second_moment, step):
    place = lax.axis_index("fsdp")
    y, z, c = place // (Z * C), place // C % Z, place % C
    master = weight[0]
    rows, cols = master.shape
    half, quarter = cols // 2, cols // 4
    factor = D ** (-0.5)

    wire = master.astype(BF)
    mine = lax.dynamic_slice_in_dim(wire, c * half, half, 1)
    theirs = lax.dynamic_slice_in_dim(wire, (1 - c) * half, half, 1)
    block = ordered(c, mine, hop(theirs, dc=1))

    widened = tokens.astype(F32)
    scale = lax.rsqrt(jnp.mean(widened * widened, axis=1, keepdims=True) + 1e-06)
    cot_mine = lax.dynamic_slice_in_dim(cotangent, c * half, half, 1)
    cot_theirs = lax.dynamic_slice_in_dim(cotangent, (1 - c) * half, half, 1)
    cot = jnp.concatenate([cot_mine, hop(cot_theirs, dc=1)], axis=0)
    width = rows * Z * C
    normed, terms = {}, {}
    for k in (2, 1, 3, 0):
        part = lax.dynamic_slice_in_dim(tokens, (y + k) % Y * width, width, 1)
        part = (part.astype(F32) * scale).astype(BF)
        normed[k] = jnp.concatenate([part, hop(part, dc=1)], axis=0)
        terms[k] = lax.dot_general(
            normed[k], cot, (((0,), (0,)), ((), ())), preferred_element_type=F32
        ).astype(BF)

    tall = rows * C

    def along_y(part):
        mid = part[2].shape[0] // 2
        low = hop(part[2][:mid], dy=1)
        high = hop(part[2][mid:], dy=-1)
        up = jnp.concatenate([part[1][:mid] + low, part[1][mid:]], axis=0)
        down = jnp.concatenate([part[3][:mid], part[3][mid:] + high], axis=0)
        from_below = hop(up, dy=1)
        from_above = hop(down, dy=-1)
        return part[0].astype(F32) + from_below.astype(F32) + from_above.astype(F32)

    def along_z(value):
        mine = rows_of(value, z * tall, tall)
        theirs = rows_of(value, (1 - z) * tall, tall)
        return mine, hop(theirs.astype(BF), dz=1)

    mine, other = {}, {}
    for k in (2, 1, 3, 0):
        mine[k], other[k] = along_z(terms[k][:, quarter:])
    sum_b = along_y({k: mine[k] + other[k] for k in mine})
    part_a, from_z = along_z(along_y({k: terms[k][:, :quarter] for k in terms}))
    sum_a = part_a + from_z.astype(F32)

    def to_owner(value):
        mine = rows_of(value, c * rows, rows)
        theirs = rows_of(value, (1 - c) * rows, rows).astype(BF)
        return ordered(c, mine[:, None], hop(theirs, dc=1).astype(F32)[:, None], axis=1)

    grad = jnp.concatenate([to_owner(sum_a), to_owner(sum_b)], axis=2).reshape(rows, cols) * factor

    def gather_y(own):
        mid = own.shape[0] // 2
        below = hop(own, dy=1)
        above = hop(own, dy=-1)
        low = hop(below[:mid], dy=1)
        high = hop(above[mid:], dy=-1)
        return {0: own, 1: above, 3: below, 2: jnp.concatenate([low, high], axis=0)}

    block_a, block_b = block[:, :quarter], block[:, quarter:]
    whole_b = gather_y(ordered(z, block_b, hop(block_b, dz=1)))
    line_a = gather_y(block_a)
    whole_a = {k: ordered(z, line_a[k], hop(line_a[k], dz=1)) for k in (0, 1, 3, 2)}
    projected = [0.0, 0.0]
    for k in (0, 1, 3, 2):
        for which, whole in enumerate((whole_a, whole_b)):
            projected[which] += jnp.dot(normed[k], whole[k], preferred_element_type=F32)
    result = (jnp.concatenate(projected, axis=1) * factor).astype(BF)
    count = tokens.shape[0]
    values = ordered(c, result[:count], hop(result[count:], dc=1), axis=1)

    new_first = 0.9 * first_moment[0] + 0.1 * grad
    new_second = 0.999 * second_moment[0] + 0.001 * grad * grad
    time = (step[0] + 1).astype(F32)
    corr_one = 1.0 - jnp.exp(time * jnp.log(F32(0.9)))
    corr_two = 1.0 - jnp.exp(time * jnp.log(F32(0.999)))
    change = new_first / corr_one / (jnp.sqrt(new_second / corr_two) + 1e-08)
    updated = master - 0.02 * (change + 0.1 * master)
    levels = lax.axis_size("peer").bit_length() - 1
    partner = lax.switch(
        step[0] % levels, [partial(gossip, bit=which) for which in range(levels)], updated.astype(BF)
    )
    averaged = 0.5 * (updated + partner.astype(F32))
    return (values, averaged[None], new_first[None], new_second[None])


def solution(mesh):
    return jax.shard_map(
        on_device,
        mesh=mesh,
        in_specs=(
            P(("peer", "fsdp"), None),
            P(("peer", "fsdp"), None),
            P("peer", "fsdp", None),
            P("peer", "fsdp", None),
            P("peer", "fsdp", None),
            P(),
        ),
        out_specs=(
            P(("peer", "fsdp"), None),
            P("peer", "fsdp", None),
            P("peer", "fsdp", None),
            P("peer", "fsdp", None),
        ),
        check_vma=False,
    )
```

```python
from functools import partial

import jax
import jax.numpy as jnp
from jax import lax
from jax.experimental import pallas as pl
from jax.experimental.pallas import tpu as pltpu
from jax.sharding import PartitionSpec as P

D = 4608
Y, Z, C = 4, 2, 2
BF, F32 = jnp.bfloat16, jnp.float32
MIB = 2**20


def hop(value, dy=0, dz=0, dc=0):
    pairs = []
    for i in range(Y * Z * C):
        y, z, c = i // (Z * C), i // C % Z, i % C
        pairs.append((i, ((y + dy) % Y * Z + (z ^ dz)) * C + (c ^ dc)))
    return lax.ppermute(value, "fsdp", pairs)


def gossip(value, bit):
    mask = 2**bit
    pairs = [(source, source ^ mask) for source in range(lax.axis_size("peer"))]
    return lax.ppermute(value, "peer", pairs)


def where():
    index = lax.axis_index("fsdp")
    return index // (Z * C), index // C % Z, index % C


def pick(bit, first, second):
    return jnp.where(bit == 0, first, second)


def after(values, *earlier):
    return lax.optimization_barrier(tuple(values) + earlier)[: len(values)]


def shape(dtype, *dims):
    return jax.ShapeDtypeStruct(dims, dtype)


def kernel_call(kernel, ins, outs, scratch=(), limit=16, flops=0):
    moved = sum(a.size * a.dtype.itemsize for a in (*ins, *outs))
    return pl.pallas_call(
        kernel,
        in_specs=[pl.BlockSpec(memory_space=pltpu.VMEM)] * len(ins),
        out_specs=[pl.BlockSpec(memory_space=pltpu.VMEM)] * len(outs),
        out_shape=list(outs),
        scratch_shapes=list(scratch),
        compiler_params=pltpu.CompilerParams(vmem_limit_bytes=limit * MIB),
        cost_estimate=pl.CostEstimate(flops=flops, bytes_accessed=moved, transcendentals=0),
    )(*ins)


def dot(left, right):
    return jnp.dot(left, right, preferred_element_type=F32)


def dot_rows(left, right):
    return lax.dot_general(left, right, (((0,), (0,)), ((), ())), preferred_element_type=F32)


def norm_kernel(tokens, norm_2, norm_r):
    y, _, _ = where()
    width = norm_2.shape[1]
    squares = 0.0
    for i in range(tokens.shape[1] // 128):
        part = tokens[:, i * 128 : (i + 1) * 128].astype(F32)
        squares += part * part
    scale = lax.rsqrt(jnp.sum(squares, axis=1, keepdims=True) / D + 1e-06)
    for slot, k in enumerate((2, 1, 3, 0)):
        start = pl.multiple_of(lax.rem(y + k, Y) * width, 128)
        part = (tokens[:, pl.ds(start, width)].astype(F32) * scale).astype(BF)
        if slot == 0:
            norm_2[...] = part
        else:
            norm_r[slot - 1] = part


def normalise(tokens):
    count, width = tokens.shape[0], tokens.shape[1] // Y
    tile = count // 4
    return pl.pallas_call(
        norm_kernel,
        grid=(4,),
        in_specs=[pl.BlockSpec((tile, tokens.shape[1]), lambda i: (i, 0))],
        out_specs=[
            pl.BlockSpec((tile, width), lambda i: (i, 0)),
            pl.BlockSpec((3, tile, width), lambda i: (0, i, 0)),
        ],
        out_shape=[shape(BF, count, width), shape(BF, 3, count, width)],
        cost_estimate=pl.CostEstimate(flops=0, bytes_accessed=4 * tokens.size, transcendentals=0),
    )(tokens)


def term(mine, theirs, cot_mine, cot_theirs, product):
    width = mine.shape[1]
    tile = width // 3
    for i in range(3):
        here = slice(i * tile, (i + 1) * tile)
        product[here, :] = (
            dot_rows(mine[:, here], cot_mine[...]) + dot_rows(theirs[:, here], cot_theirs[...])
        ).astype(BF)


def term_2_kernel(mine, theirs, cot_mine, cot_theirs, low, high, near, far, product):
    (_, z, _), tall, quarter = where(), low.shape[0], low.shape[1]
    term(mine, theirs, cot_mine, cot_theirs, product)
    low[...] = product[:tall, :quarter]
    high[...] = product[tall:, :quarter]
    near[...] = pick(z, product[:tall, quarter:], product[tall:, quarter:])
    far[...] = pick(z, product[tall:, quarter:], product[:tall, quarter:])


def term_r_kernel(mine, theirs, cot_mine, cot_theirs, part_a, near, far, product):
    (_, z, _), tall, quarter = where(), near.shape[1], near.shape[2]

    def step(k, carry):
        term(mine.at[k], theirs.at[k], cot_mine, cot_theirs, product)
        part_a[k] = product[:, :quarter]
        near[k] = pick(z, product[:tall, quarter:], product[tall:, quarter:])
        far[k] = pick(z, product[tall:, quarter:], product[:tall, quarter:])
        return carry

    lax.fori_loop(0, 3, step, 0)


def scatter_2_kernel(part_a, low, high, near, got, up, down):
    tall = low.shape[0]
    wide, mid = 2 * tall, tall // 2
    up[:tall] = part_a[0, :tall] + low[...]
    up[tall:wide] = part_a[0, tall:]
    up[wide:] = near[:mid] + got[:mid]
    down[:tall] = part_a[1, :tall]
    down[tall:wide] = part_a[1, tall:] + high[...]
    down[wide:] = near[mid:] + got[mid:]


def scatter_3_kernel(part_a, near, below, above, got, up, down, far_a, near_a, sum_b, total):
    (_, z, _), tall = where(), far_a.shape[0]
    wide, mid = 2 * tall, tall // 2
    up[:mid] = near[0, :mid] + got[0, :mid] + below[wide:]
    up[mid:] = near[0, mid:] + got[0, mid:]
    down[:mid] = near[1, :mid] + got[1, :mid]
    down[mid:] = near[1, mid:] + got[1, mid:] + above[wide:]
    sum_b[...] = near[2].astype(F32) + got[2].astype(F32)
    total[...] = part_a[2].astype(F32) + below[:wide].astype(F32) + above[:wide].astype(F32)
    near_a[...] = pick(z, total[:tall], total[tall:])
    far_a[...] = pick(z, total[tall:], total[:tall]).astype(BF)


def scatter_4_kernel(near_a, last_z, sum_b, below, above, own, theirs, total):
    (_, _, c), rows, quarter = where(), own.shape[0], near_a.shape[1]
    total[:, :quarter] = near_a[...] + last_z[...].astype(F32)
    total[:, quarter:] = sum_b[...] + below[...].astype(F32) + above[...].astype(F32)
    own[...] = pick(c, total[:rows], total[rows:])
    theirs[...] = pick(c, total[rows:], total[:rows]).astype(BF)


def gather_1_kernel(mine, theirs, block_a, block_b):
    (_, _, c), rows, quarter = where(), mine.shape[0], block_a.shape[1]
    first, second = pick(c, mine[...], theirs[...]), pick(c, theirs[...], mine[...])
    block_a[:rows], block_b[:rows] = first[:, :quarter], first[:, quarter:]
    block_a[rows:], block_b[rows:] = second[:, :quarter], second[:, quarter:]


def gather_2_kernel(block_a, block_b, block_z, above, below, up, down, along):
    (_, z, _), tall = where(), block_a.shape[0]
    wide, mid = 2 * tall, tall // 2
    for out in (up, down):
        out[:tall] = pick(z, block_b[...], block_z[...])
        out[tall:wide] = pick(z, block_z[...], block_b[...])
    up[wide:] = below[:mid]
    down[wide:] = above[mid:]
    along[0] = above[...]
    along[1] = below[...]
    along[2] = block_a[...]


def gather_3_kernel(got_up, got_down, up, down, line):
    tall = line.shape[0]
    wide, mid = 2 * tall, tall // 2
    up[...] = got_up[:tall]
    down[...] = got_down[tall:wide]
    line[:mid] = got_up[wide:]
    line[mid:] = got_down[wide:]


def project(mine, theirs, whole, total):
    count = mine.shape[0]
    total[:count] += dot(mine, whole)
    total[count:] += dot(theirs, whole)


def order_z(z, own, other, whole):
    tall, quarter = own.shape
    whole[:tall, :quarter] = pick(z, own, other)
    whole[tall:, :quarter] = pick(z, other, own)


def project_r_kernel(mine, theirs, along, got_z, own_up, got_up, got_down, total, whole):
    _, z, _ = where()
    wide, quarter = whole.shape[0], got_up.shape[1]
    total[...] = jnp.zeros_like(total)
    for k, part in enumerate((got_down, got_up, own_up)):
        order_z(z, along[k], got_z[k], whole)
        whole[:, quarter:] = part[:wide]
        project(mine[k], theirs[k], whole[...], total)


def project_2_kernel(mine, theirs, line, got_z, low, high, before, own, other, whole, total):
    _, z, _ = where()
    tall, quarter = line.shape
    count = own.shape[0]
    order_z(z, line[...], got_z[...], whole)
    whole[:tall, quarter:] = low[...]
    whole[tall:, quarter:] = high[...]
    total[...] = before[...]
    project(mine[...], theirs[...], whole[...], total)
    own[...] = (total[:count] * D ** (-0.5)).astype(BF)
    other[...] = (total[count:] * D ** (-0.5)).astype(BF)


def place_kernel(own, other, values):
    (_, _, c), half = where(), own.shape[1]
    values[:, :half] = pick(c, own[...], other[...])
    values[:, half:] = pick(c, other[...], own[...])


def adam_kernel(rates, mine, other, master, first, second, new_first, new_second, updated, wire):
    (_, _, c), half = where(), mine.shape[1]

    def rows(i, carry):
        here = pl.ds(pl.multiple_of(i * 16, 16), 16)
        for j in range(2):
            there = slice(j * half, (j + 1) * half)
            grad = jnp.where(c == j, mine[here, :], other[here, :].astype(F32)) * D ** (-0.5)
            moment = 0.9 * first[0, here, there] + 0.1 * grad
            square = 0.999 * second[0, here, there] + 0.001 * grad * grad
            scaled = square * rates[1]
            root = scaled * lax.rsqrt(scaled) + 1e-08
            guess = pl.reciprocal(root, approx=True)
            change = moment * rates[0] * (guess * (2.0 - root * guess))
            old = master[0, here, there]
            result = old - 0.02 * (change + 0.1 * old)
            new_first[0, here, there] = moment
            new_second[0, here, there] = square
            updated[here, there] = result
            wire[here, there] = result.astype(BF)
        return carry

    lax.fori_loop(0, mine.shape[0] // 16, rows, 0, unroll=2)


def adam(step, mine, other, master, first, second):
    _, rows, cols = master.shape
    half, tile = cols // 2, rows // 3
    time = (step[0] + 1).astype(F32)
    rate_one = 1.0 - jnp.exp(time * jnp.log(F32(0.9)))
    rate_two = 1.0 - jnp.exp(time * jnp.log(F32(0.999)))
    rates = jnp.stack([1.0 / rate_one, 1.0 / rate_two])
    part = pl.BlockSpec((tile, half), lambda i: (i, 0))
    full = pl.BlockSpec((1, tile, cols), lambda i: (0, i, 0))
    flat = pl.BlockSpec((tile, cols), lambda i: (i, 0))
    scalar = pl.BlockSpec(memory_space=pltpu.SMEM)
    return pl.pallas_call(
        adam_kernel,
        grid=(3,),
        in_specs=[scalar, part, part, full, full, full],
        out_specs=[full, full, flat, flat],
        out_shape=[
            shape(F32, 1, rows, cols),
            shape(F32, 1, rows, cols),
            shape(F32, rows, cols),
            shape(BF, rows, cols),
        ],
        cost_estimate=pl.CostEstimate(flops=20 * rows * cols, bytes_accessed=30 * rows * cols, transcendentals=0),
    )(rates, mine, other, master, first, second)


def on_device(tokens, cotangent, weight, first_moment, second_moment, step):
    _, _, c = where()
    master = weight[0]
    rows, cols = master.shape
    half, quarter, tall = cols // 2, cols // 4, rows * C
    wide, mid = 2 * tall, tall // 2
    tokens_here = tokens.shape[0]

    theirs = lax.dynamic_slice_in_dim(master, (1 - c) * half, half, 1).astype(BF)
    mine = lax.dynamic_slice_in_dim(master, c * half, half, 1).astype(BF)
    theirs = hop(theirs, dc=1)
    block = shape(BF, tall, quarter)
    block_a, block_b = kernel_call(gather_1_kernel, (mine, theirs), (block, block), limit=8)
    above = hop(block_a, dy=-1)
    below = hop(block_a, dy=1)
    block_z = hop(block_b, dz=1)

    cot_mine = lax.dynamic_slice_in_dim(cotangent, c * half, half, 1)
    cot_theirs = hop(lax.dynamic_slice_in_dim(cotangent, (1 - c) * half, half, 1), dc=1)
    norm_2, norm_r = normalise(tokens)
    (send_2,) = after((norm_2,), theirs, cot_theirs)
    far_2 = hop(send_2, dc=1)
    (send_r,) = after((norm_r,), far_2)
    far_r = hop(send_r, dc=1)
    product = pltpu.VMEM((wide, half), BF)
    low, high, near_2, got_2 = kernel_call(
        term_2_kernel,
        (norm_2, far_2, cot_mine, cot_theirs),
        (block,) * 4,
        (product,),
        limit=12,
        flops=4 * tokens_here * wide * half,
    )
    three = shape(BF, 3, tall, quarter)
    part_a, near_r, got_r = kernel_call(
        term_r_kernel,
        (norm_r, far_r, cot_mine, cot_theirs),
        (shape(BF, 3, wide, quarter), three, three),
        (product,),
        limit=20,
        flops=12 * tokens_here * wide * half,
    )

    low, high, got_2 = after((low, high, got_2), block_a, block_b)
    low = hop(low, dy=1)
    high = hop(high, dy=-1)
    got_2 = hop(got_2, dz=1)
    got_r = hop(got_r, dz=1)
    long = shape(BF, wide + mid, quarter)
    part_a, low, high, near_2, got_2 = after((part_a, low, high, near_2, got_2), above, below, block_z)
    up, down = kernel_call(scatter_2_kernel, (part_a, low, high, near_2, got_2), (long, long))
    from_below = hop(up, dy=1)
    from_above = hop(down, dy=-1)
    block_f = shape(F32, tall, quarter)
    up, down, far_a, near_a, sum_b = kernel_call(
        scatter_3_kernel,
        (part_a, near_r, from_below, from_above, got_r),
        (block, block, block, block_f, block_f),
        (pltpu.VMEM((wide, quarter), F32),),
    )
    last_below = hop(up, dy=1)
    last_above = hop(down, dy=-1)
    last_z = hop(far_a, dz=1)
    own, other = kernel_call(
        scatter_4_kernel,
        (near_a, last_z, sum_b, last_below, last_above),
        (shape(F32, rows, half), shape(BF, rows, half)),
        (pltpu.VMEM((tall, half), F32),),
        limit=12,
    )
    other = hop(other, dc=1)

    up, down, along = kernel_call(
        gather_2_kernel, (block_a, block_b, block_z, above, below), (long, long, three)
    )
    up, down, along = after((up, down, along), last_below, last_above, last_z)
    got_up = hop(up, dy=1)
    got_down = hop(down, dy=-1)
    got_z = hop(along, dz=1)
    new_first, new_second, updated, wire = adam(step, own, other, weight, first_moment, second_moment)
    got_up, got_down = after((got_up, got_down), wire)
    last_up, last_down, line = kernel_call(
        gather_3_kernel, (got_up, got_down), (block, block, block), limit=8
    )
    last_up = hop(last_up, dy=1)
    last_down = hop(last_down, dy=-1)
    line_z = hop(line, dz=1)

    whole = pltpu.VMEM((wide, half), BF)
    (total,) = kernel_call(
        project_r_kernel,
        (norm_r, far_r, along, got_z, up, got_up, got_down),
        (shape(F32, 2 * tokens_here, half),),
        (whole,),
        limit=20,
        flops=12 * tokens_here * wide * half,
    )
    result = shape(BF, tokens_here, half)
    result_own, result_other = kernel_call(
        project_2_kernel,
        (norm_2, far_2, line, line_z, last_up, last_down, total),
        (result, result),
        (whole, pltpu.VMEM((2 * tokens_here, half), F32)),
        limit=16,
        flops=4 * tokens_here * wide * half,
    )
    (values,) = kernel_call(
        place_kernel, (result_own, hop(result_other, dc=1)), (shape(BF, tokens_here, cols),), limit=8
    )

    levels = lax.axis_size("peer").bit_length() - 1
    partner = lax.switch(step[0] % levels, [partial(gossip, bit=which) for which in range(levels)], wire)
    averaged = 0.5 * (updated + partner.astype(F32))
    return (values, averaged[None], new_first, new_second)


def solution(mesh):
    return jax.shard_map(
        on_device,
        mesh=mesh,
        in_specs=(
            P(("peer", "fsdp"), None),
            P(("peer", "fsdp"), None),
            P("peer", "fsdp", None),
            P("peer", "fsdp", None),
            P("peer", "fsdp", None),
            P(),
        ),
        out_specs=(
            P(("peer", "fsdp"), None),
            P("peer", "fsdp", None),
            P("peer", "fsdp", None),
            P("peer", "fsdp", None),
        ),
        check_vma=False,
    )
```

```python
from functools import partial

import jax
import jax.numpy as jnp
from jax import lax
from jax.experimental import pallas as pl
from jax.experimental.pallas import tpu as pltpu
from jax.sharding import PartitionSpec as P

D = 4608
Y, Z, C = 4, 2, 2
BF, F32 = jnp.bfloat16, jnp.float32
MIB = 2**20


def hop(value, dy=0, dz=0, dc=0):
    pairs = []
    for i in range(Y * Z * C):
        y, z, c = i // (Z * C), i // C % Z, i % C
        pairs.append((i, ((y + dy) % Y * Z + (z ^ dz)) * C + (c ^ dc)))
    return lax.ppermute(value, "fsdp", pairs)


def gossip(value, bit):
    mask = 2**bit
    pairs = [(source, source ^ mask) for source in range(lax.axis_size("peer"))]
    return lax.ppermute(value, "peer", pairs)


def where():
    index = lax.axis_index("fsdp")
    return index // (Z * C), index // C % Z, index % C


def pick(bit, first, second):
    return jnp.where(bit == 0, first, second)


def after(values, *earlier):
    return lax.optimization_barrier(tuple(values) + earlier)[: len(values)]


def shape(dtype, *dims):
    return jax.ShapeDtypeStruct(dims, dtype)


def kernel_call(kernel, ins, outs, scratch=(), limit=16, flops=0):
    moved = sum(a.size * a.dtype.itemsize for a in (*ins, *outs))
    return pl.pallas_call(
        kernel,
        in_specs=[pl.BlockSpec(memory_space=pltpu.VMEM)] * len(ins),
        out_specs=[pl.BlockSpec(memory_space=pltpu.VMEM)] * len(outs),
        out_shape=list(outs),
        scratch_shapes=list(scratch),
        compiler_params=pltpu.CompilerParams(vmem_limit_bytes=limit * MIB),
        cost_estimate=pl.CostEstimate(flops=flops, bytes_accessed=moved, transcendentals=0),
    )(*ins)


def dot(left, right):
    return jnp.dot(left, right, preferred_element_type=F32)


def dot_rows(left, right):
    return lax.dot_general(left, right, (((0,), (0,)), ((), ())), preferred_element_type=F32)


def norm_kernel(tokens, norm_2, norm_r, rows, sems):
    y, _, _ = where()
    width, tile = norm_2.shape[1], rows.shape[1]
    copies = [
        pltpu.make_async_copy(tokens.at[pl.ds(t * tile, tile), :], rows.at[t], sems.at[t])
        for t in range(rows.shape[0])
    ]
    for copy in copies:
        copy.start()
    for t, copy in enumerate(copies):
        here = slice(t * tile, (t + 1) * tile)
        copy.wait()
        squares = 0.0
        for i in range(tokens.shape[1] // 128):
            part = rows[t, :, i * 128 : (i + 1) * 128].astype(F32)
            squares += part * part
        scale = lax.rsqrt(jnp.sum(squares, axis=1, keepdims=True) / D + 1e-06)
        for slot, k in enumerate((2, 1, 3, 0)):
            start = pl.multiple_of(lax.rem(y + k, Y) * width, 128)
            part = (rows[t, :, pl.ds(start, width)].astype(F32) * scale).astype(BF)
            if slot == 0:
                norm_2[here, :] = part
            else:
                norm_r[slot - 1, here, :] = part


def normalise(tokens):
    count, width = tokens.shape[0], tokens.shape[1] // Y
    tiles = 8
    return pl.pallas_call(
        norm_kernel,
        in_specs=[pl.BlockSpec(memory_space=pl.ANY)],
        out_specs=[pl.BlockSpec(memory_space=pltpu.VMEM)] * 2,
        out_shape=[shape(BF, count, width), shape(BF, 3, count, width)],
        scratch_shapes=[
            pltpu.VMEM((tiles, count // tiles, tokens.shape[1]), BF),
            pltpu.SemaphoreType.DMA((tiles,)),
        ],
        compiler_params=pltpu.CompilerParams(vmem_limit_bytes=12 * MIB),
        cost_estimate=pl.CostEstimate(flops=0, bytes_accessed=4 * tokens.size, transcendentals=0),
    )(tokens)


def term(mine, theirs, cot_mine, cot_theirs, product):
    width = mine.shape[1]
    tile = width // 3
    for i in range(3):
        here = slice(i * tile, (i + 1) * tile)
        product[here, :] = (
            dot_rows(mine[:, here], cot_mine[...]) + dot_rows(theirs[:, here], cot_theirs[...])
        ).astype(BF)


def term_2_kernel(mine, theirs, cot_mine, cot_theirs, low, high, near, far, product):
    (_, z, _), tall, quarter = where(), low.shape[0], low.shape[1]
    term(mine, theirs, cot_mine, cot_theirs, product)
    low[...] = product[:tall, :quarter]
    high[...] = product[tall:, :quarter]
    near[...] = pick(z, product[:tall, quarter:], product[tall:, quarter:])
    far[...] = pick(z, product[tall:, quarter:], product[:tall, quarter:])


def term_r_kernel(mine, theirs, cot_mine, cot_theirs, part_a, near, far, product):
    (_, z, _), tall, quarter = where(), near.shape[1], near.shape[2]

    def step(k, carry):
        term(mine.at[k], theirs.at[k], cot_mine, cot_theirs, product)
        part_a[k] = product[:, :quarter]
        near[k] = pick(z, product[:tall, quarter:], product[tall:, quarter:])
        far[k] = pick(z, product[tall:, quarter:], product[:tall, quarter:])
        return carry

    lax.fori_loop(0, 3, step, 0)


def scatter_2_kernel(part_a, low, high, near, got, up, down):
    tall = low.shape[0]
    wide, mid = 2 * tall, tall // 2
    up[:tall] = part_a[0, :tall] + low[...]
    up[tall:wide] = part_a[0, tall:]
    up[wide:] = near[:mid] + got[:mid]
    down[:tall] = part_a[1, :tall]
    down[tall:wide] = part_a[1, tall:] + high[...]
    down[wide:] = near[mid:] + got[mid:]


def scatter_3_kernel(part_a, near, below, above, got, up, down, far_a, near_a, sum_b, total):
    (_, z, _), tall = where(), far_a.shape[0]
    wide, mid = 2 * tall, tall // 2
    up[:mid] = near[0, :mid] + got[0, :mid] + below[wide:]
    up[mid:] = near[0, mid:] + got[0, mid:]
    down[:mid] = near[1, :mid] + got[1, :mid]
    down[mid:] = near[1, mid:] + got[1, mid:] + above[wide:]
    sum_b[...] = near[2].astype(F32) + got[2].astype(F32)
    total[...] = part_a[2].astype(F32) + below[:wide].astype(F32) + above[:wide].astype(F32)
    near_a[...] = pick(z, total[:tall], total[tall:])
    far_a[...] = pick(z, total[tall:], total[:tall]).astype(BF)


def scatter_4_kernel(near_a, last_z, sum_b, below, above, own, theirs, total):
    (_, _, c), rows, quarter = where(), own.shape[0], near_a.shape[1]
    total[:, :quarter] = near_a[...] + last_z[...].astype(F32)
    total[:, quarter:] = sum_b[...] + below[...].astype(F32) + above[...].astype(F32)
    own[...] = pick(c, total[:rows], total[rows:])
    theirs[...] = pick(c, total[rows:], total[:rows]).astype(BF)


def gather_1_kernel(mine, theirs, block_a, block_b):
    (_, _, c), rows, quarter = where(), mine.shape[0], block_a.shape[1]
    first, second = pick(c, mine[...], theirs[...]), pick(c, theirs[...], mine[...])
    block_a[:rows], block_b[:rows] = first[:, :quarter], first[:, quarter:]
    block_a[rows:], block_b[rows:] = second[:, :quarter], second[:, quarter:]


def gather_2_kernel(block_a, block_b, block_z, above, below, up, down, along):
    (_, z, _), tall = where(), block_a.shape[0]
    wide, mid = 2 * tall, tall // 2
    for out in (up, down):
        out[:tall] = pick(z, block_b[...], block_z[...])
        out[tall:wide] = pick(z, block_z[...], block_b[...])
    up[wide:] = below[:mid]
    down[wide:] = above[mid:]
    along[0] = above[...]
    along[1] = below[...]
    along[2] = block_a[...]


def gather_3_kernel(got_up, got_down, up, down, line):
    tall = line.shape[0]
    wide, mid = 2 * tall, tall // 2
    up[...] = got_up[:tall]
    down[...] = got_down[tall:wide]
    line[:mid] = got_up[wide:]
    line[mid:] = got_down[wide:]


def project(mine, theirs, whole, total):
    count = mine.shape[0]
    total[:count] += dot(mine, whole)
    total[count:] += dot(theirs, whole)


def order_z(z, own, other, whole):
    tall, quarter = own.shape
    whole[:tall, :quarter] = pick(z, own, other)
    whole[tall:, :quarter] = pick(z, other, own)


def project_r_kernel(mine, theirs, along, got_z, own_up, got_up, got_down, total, whole):
    _, z, _ = where()
    wide, quarter = whole.shape[0], got_up.shape[1]
    total[...] = jnp.zeros_like(total)
    for k, part in enumerate((got_down, got_up, own_up)):
        order_z(z, along[k], got_z[k], whole)
        whole[:, quarter:] = part[:wide]
        project(mine[k], theirs[k], whole[...], total)


def project_2_kernel(mine, theirs, line, got_z, low, high, before, own, other, whole, total):
    _, z, _ = where()
    tall, quarter = line.shape
    count = own.shape[0]
    order_z(z, line[...], got_z[...], whole)
    whole[:tall, quarter:] = low[...]
    whole[tall:, quarter:] = high[...]
    total[...] = before[...]
    project(mine[...], theirs[...], whole[...], total)
    own[...] = (total[:count] * D ** (-0.5)).astype(BF)
    other[...] = (total[count:] * D ** (-0.5)).astype(BF)


def place_kernel(own, other, values):
    (_, _, c), half = where(), own.shape[1]
    values[:, :half] = pick(c, own[...], other[...])
    values[:, half:] = pick(c, other[...], own[...])


def adam_kernel(rates, mine, other, master, first, second, new_first, new_second, updated, wire):
    (_, _, c), half = where(), mine.shape[1]

    def rows(i, carry):
        here = pl.ds(pl.multiple_of(i * 16, 16), 16)
        for j in range(2):
            there = slice(j * half, (j + 1) * half)
            grad = jnp.where(c == j, mine[here, :], other[here, :].astype(F32)) * D ** (-0.5)
            moment = 0.9 * first[0, here, there] + 0.1 * grad
            square = 0.999 * second[0, here, there] + 0.001 * grad * grad
            scaled = square * rates[1]
            root = scaled * lax.rsqrt(scaled) + 1e-08
            guess = pl.reciprocal(root, approx=True)
            change = moment * rates[0] * (guess * (2.0 - root * guess))
            old = master[0, here, there]
            result = old - 0.02 * (change + 0.1 * old)
            new_first[0, here, there] = moment
            new_second[0, here, there] = square
            updated[here, there] = result
            wire[here, there] = result.astype(BF)
        return carry

    lax.fori_loop(0, mine.shape[0] // 16, rows, 0, unroll=2)


def adam(step, mine, other, master, first, second):
    _, rows, cols = master.shape
    half, tile = cols // 2, rows // 3
    time = (step[0] + 1).astype(F32)
    rate_one = 1.0 - jnp.exp(time * jnp.log(F32(0.9)))
    rate_two = 1.0 - jnp.exp(time * jnp.log(F32(0.999)))
    rates = jnp.stack([1.0 / rate_one, 1.0 / rate_two])
    part = pl.BlockSpec((tile, half), lambda i: (i, 0))
    full = pl.BlockSpec((1, tile, cols), lambda i: (0, i, 0))
    flat = pl.BlockSpec((tile, cols), lambda i: (i, 0))
    scalar = pl.BlockSpec(memory_space=pltpu.SMEM)
    return pl.pallas_call(
        adam_kernel,
        grid=(3,),
        in_specs=[scalar, part, part, full, full, full],
        out_specs=[full, full, flat, flat],
        out_shape=[
            shape(F32, 1, rows, cols),
            shape(F32, 1, rows, cols),
            shape(F32, rows, cols),
            shape(BF, rows, cols),
        ],
        cost_estimate=pl.CostEstimate(flops=20 * rows * cols, bytes_accessed=30 * rows * cols, transcendentals=0),
    )(rates, mine, other, master, first, second)


def on_device(tokens, cotangent, weight, first_moment, second_moment, step):
    _, _, c = where()
    master = weight[0]
    rows, cols = master.shape
    half, quarter, tall = cols // 2, cols // 4, rows * C
    wide, mid = 2 * tall, tall // 2
    tokens_here = tokens.shape[0]

    cot_mine = lax.dynamic_slice_in_dim(cotangent, c * half, half, 1)
    cot_theirs = hop(lax.dynamic_slice_in_dim(cotangent, (1 - c) * half, half, 1), dc=1)
    norm_2, norm_r = normalise(tokens)
    far_2 = hop(norm_2, dc=1)

    block = shape(BF, tall, quarter)
    product = pltpu.VMEM((wide, half), BF)
    low, high, near_2, got_2 = kernel_call(
        term_2_kernel,
        (norm_2, far_2, cot_mine, cot_theirs),
        (block,) * 4,
        (product,),
        limit=12,
        flops=4 * tokens_here * wide * half,
    )
    (send_r,) = after((norm_r,), low)
    far_r = hop(send_r, dc=1)
    three = shape(BF, 3, tall, quarter)
    part_a, near_r, got_r = kernel_call(
        term_r_kernel,
        (norm_r, far_r, cot_mine, cot_theirs),
        (shape(BF, 3, wide, quarter), three, three),
        (product,),
        limit=20,
        flops=12 * tokens_here * wide * half,
    )

    theirs = lax.dynamic_slice_in_dim(master, (1 - c) * half, half, 1).astype(BF)
    mine = lax.dynamic_slice_in_dim(master, c * half, half, 1).astype(BF)
    (theirs,) = after((theirs,), low)
    theirs = hop(theirs, dc=1)
    block_a, block_b = kernel_call(gather_1_kernel, (mine, theirs), (block, block), limit=8)
    low = hop(low, dy=1)
    high = hop(high, dy=-1)
    got_2 = hop(got_2, dz=1)
    got_r = hop(got_r, dz=1)
    long = shape(BF, wide + mid, quarter)
    up, down = kernel_call(scatter_2_kernel, (part_a, low, high, near_2, got_2), (long, long))
    send_a, send_b = after((block_a, block_b), up, down)
    from_below = hop(up, dy=1)
    from_above = hop(down, dy=-1)
    above = hop(send_a, dy=-1)
    below = hop(send_a, dy=1)
    block_z = hop(send_b, dz=1)
    block_f = shape(F32, tall, quarter)
    up, down, far_a, near_a, sum_b = kernel_call(
        scatter_3_kernel,
        (part_a, near_r, from_below, from_above, got_r),
        (block, block, block, block_f, block_f),
        (pltpu.VMEM((wide, quarter), F32),),
    )
    last_below = hop(up, dy=1)
    last_above = hop(down, dy=-1)
    last_z = hop(far_a, dz=1)
    own, other = kernel_call(
        scatter_4_kernel,
        (near_a, last_z, sum_b, last_below, last_above),
        (shape(F32, rows, half), shape(BF, rows, half)),
        (pltpu.VMEM((tall, half), F32),),
        limit=12,
    )
    other = hop(other, dc=1)

    up, down, along = kernel_call(
        gather_2_kernel, (block_a, block_b, block_z, above, below), (long, long, three)
    )
    up, down, along = after((up, down, along), last_below, last_above, last_z)
    got_up = hop(up, dy=1)
    got_down = hop(down, dy=-1)
    got_z = hop(along, dz=1)
    new_first, new_second, updated, wire = adam(step, own, other, weight, first_moment, second_moment)
    levels = lax.axis_size("peer").bit_length() - 1
    partner = lax.switch(step[0] % levels, [partial(gossip, bit=which) for which in range(levels)], wire)
    got_up, got_down = after((got_up, got_down), partner)
    last_up, last_down, line = kernel_call(
        gather_3_kernel, (got_up, got_down), (block, block, block), limit=8
    )
    last_up = hop(last_up, dy=1)
    last_down = hop(last_down, dy=-1)
    line_z = hop(line, dz=1)

    whole = pltpu.VMEM((wide, half), BF)
    (total,) = kernel_call(
        project_r_kernel,
        (norm_r, far_r, along, got_z, up, got_up, got_down),
        (shape(F32, 2 * tokens_here, half),),
        (whole,),
        limit=20,
        flops=12 * tokens_here * wide * half,
    )
    result = shape(BF, tokens_here, half)
    result_own, result_other = kernel_call(
        project_2_kernel,
        (norm_2, far_2, line, line_z, last_up, last_down, total),
        (result, result),
        (whole, pltpu.VMEM((2 * tokens_here, half), F32)),
        limit=16,
        flops=4 * tokens_here * wide * half,
    )
    (values,) = kernel_call(
        place_kernel, (result_own, hop(result_other, dc=1)), (shape(BF, tokens_here, cols),), limit=8
    )

    averaged = 0.5 * (updated + partner.astype(F32))
    return (values, averaged[None], new_first, new_second)


def solution(mesh):
    return jax.shard_map(
        on_device,
        mesh=mesh,
        in_specs=(
            P(("peer", "fsdp"), None),
            P(("peer", "fsdp"), None),
            P("peer", "fsdp", None),
            P("peer", "fsdp", None),
            P("peer", "fsdp", None),
            P(),
        ),
        out_specs=(
            P(("peer", "fsdp"), None),
            P("peer", "fsdp", None),
            P("peer", "fsdp", None),
            P("peer", "fsdp", None),
        ),
        check_vma=False,
    )
```

```python
from functools import partial

import jax
import jax.numpy as jnp
from jax import lax
from jax.experimental import pallas as pl
from jax.experimental.pallas import tpu as pltpu
from jax.sharding import PartitionSpec as P

D = 4608
Y, Z, C = 4, 2, 2
BF, F32 = jnp.bfloat16, jnp.float32
MIB = 2**20


def hop(value, dy=0, dz=0, dc=0):
    pairs = []
    for i in range(Y * Z * C):
        y, z, c = i // (Z * C), i // C % Z, i % C
        pairs.append((i, ((y + dy) % Y * Z + (z ^ dz)) * C + (c ^ dc)))
    return lax.ppermute(value, "fsdp", pairs)


def gossip(value, bit):
    mask = 2**bit
    pairs = [(source, source ^ mask) for source in range(lax.axis_size("peer"))]
    return lax.ppermute(value, "peer", pairs)


def where():
    index = lax.axis_index("fsdp")
    return index // (Z * C), index // C % Z, index % C


def pick(bit, first, second):
    return jnp.where(bit == 0, first, second)


def after(values, *earlier):
    return lax.optimization_barrier(tuple(values) + earlier)[: len(values)]


def shape(dtype, *dims):
    return jax.ShapeDtypeStruct(dims, dtype)


def kernel_call(kernel, ins, outs, scratch=(), limit=16, flops=0):
    moved = sum(a.size * a.dtype.itemsize for a in (*ins, *outs))
    return pl.pallas_call(
        kernel,
        in_specs=[pl.BlockSpec(memory_space=pltpu.VMEM)] * len(ins),
        out_specs=[pl.BlockSpec(memory_space=pltpu.VMEM)] * len(outs),
        out_shape=list(outs),
        scratch_shapes=list(scratch),
        compiler_params=pltpu.CompilerParams(vmem_limit_bytes=limit * MIB),
        cost_estimate=pl.CostEstimate(flops=flops, bytes_accessed=moved, transcendentals=0),
    )(*ins)


def dot(left, right):
    return jnp.dot(left, right, preferred_element_type=F32)


def dot_rows(left, right):
    return lax.dot_general(left, right, (((0,), (0,)), ((), ())), preferred_element_type=F32)


def norm_kernel(tokens, norm_2, norm_r, rows, sems):
    y, _, _ = where()
    width, tile = norm_2.shape[1], rows.shape[1]
    copies = [
        pltpu.make_async_copy(tokens.at[pl.ds(t * tile, tile), :], rows.at[t], sems.at[t])
        for t in range(rows.shape[0])
    ]
    for copy in copies:
        copy.start()
    for t, copy in enumerate(copies):
        here = slice(t * tile, (t + 1) * tile)
        copy.wait()
        squares = 0.0
        for i in range(tokens.shape[1] // 128):
            part = rows[t, :, i * 128 : (i + 1) * 128].astype(F32)
            squares += part * part
        scale = lax.rsqrt(jnp.sum(squares, axis=1, keepdims=True) / D + 1e-06)
        for slot, k in enumerate((2, 1, 3, 0)):
            start = pl.multiple_of(lax.rem(y + k, Y) * width, 128)
            part = (rows[t, :, pl.ds(start, width)].astype(F32) * scale).astype(BF)
            if slot == 0:
                norm_2[here, :] = part
            else:
                norm_r[slot - 1, here, :] = part


def normalise(tokens):
    count, width = tokens.shape[0], tokens.shape[1] // Y
    tiles = 8
    return pl.pallas_call(
        norm_kernel,
        in_specs=[pl.BlockSpec(memory_space=pl.ANY)],
        out_specs=[pl.BlockSpec(memory_space=pltpu.VMEM)] * 2,
        out_shape=[shape(BF, count, width), shape(BF, 3, count, width)],
        scratch_shapes=[
            pltpu.VMEM((tiles, count // tiles, tokens.shape[1]), BF),
            pltpu.SemaphoreType.DMA((tiles,)),
        ],
        compiler_params=pltpu.CompilerParams(vmem_limit_bytes=12 * MIB),
        cost_estimate=pl.CostEstimate(flops=0, bytes_accessed=4 * tokens.size, transcendentals=0),
    )(tokens)


def term(mine, theirs, cot_mine, cot_theirs, product):
    width = mine.shape[1]
    tile = width // 3
    for i in range(3):
        here = slice(i * tile, (i + 1) * tile)
        product[here, :] = (
            dot_rows(mine[:, here], cot_mine[...]) + dot_rows(theirs[:, here], cot_theirs[...])
        ).astype(BF)


def term_2_kernel(mine, theirs, cot_mine, cot_theirs, low, high, near, far, product):
    (_, z, _), tall, quarter = where(), low.shape[0], low.shape[1]
    term(mine, theirs, cot_mine, cot_theirs, product)
    low[...] = product[:tall, :quarter]
    high[...] = product[tall:, :quarter]
    near[...] = pick(z, product[:tall, quarter:], product[tall:, quarter:])
    far[...] = pick(z, product[tall:, quarter:], product[:tall, quarter:])


def term_r_kernel(mine, theirs, cot_mine, cot_theirs, part_a, near, far, product):
    (_, z, _), tall, quarter = where(), near.shape[1], near.shape[2]

    def step(k, carry):
        term(mine.at[k], theirs.at[k], cot_mine, cot_theirs, product)
        part_a[k] = product[:, :quarter]
        near[k] = pick(z, product[:tall, quarter:], product[tall:, quarter:])
        far[k] = pick(z, product[tall:, quarter:], product[:tall, quarter:])
        return carry

    lax.fori_loop(0, 3, step, 0)


def scatter_2_kernel(part_a, low, high, near, got, up, down):
    tall = low.shape[0]
    wide, mid = 2 * tall, tall // 2
    up[:tall] = part_a[0, :tall] + low[...]
    up[tall:wide] = part_a[0, tall:]
    up[wide:] = near[:mid] + got[:mid]
    down[:tall] = part_a[1, :tall]
    down[tall:wide] = part_a[1, tall:] + high[...]
    down[wide:] = near[mid:] + got[mid:]


def scatter_3_kernel(part_a, near, below, above, got, up, down, far_a, near_a, sum_b, total):
    (_, z, _), tall = where(), far_a.shape[0]
    wide, mid = 2 * tall, tall // 2
    up[:mid] = near[0, :mid] + got[0, :mid] + below[wide:]
    up[mid:] = near[0, mid:] + got[0, mid:]
    down[:mid] = near[1, :mid] + got[1, :mid]
    down[mid:] = near[1, mid:] + got[1, mid:] + above[wide:]
    sum_b[...] = near[2].astype(F32) + got[2].astype(F32)
    total[...] = part_a[2].astype(F32) + below[:wide].astype(F32) + above[:wide].astype(F32)
    near_a[...] = pick(z, total[:tall], total[tall:])
    far_a[...] = pick(z, total[tall:], total[:tall]).astype(BF)


def scatter_4_kernel(near_a, last_z, sum_b, below, above, own, theirs, total):
    (_, _, c), rows, quarter = where(), own.shape[0], near_a.shape[1]
    total[:, :quarter] = near_a[...] + last_z[...].astype(F32)
    total[:, quarter:] = sum_b[...] + below[...].astype(F32) + above[...].astype(F32)
    own[...] = pick(c, total[:rows], total[rows:])
    theirs[...] = pick(c, total[rows:], total[:rows]).astype(BF)


def gather_1_kernel(mine, theirs, block_a, block_b):
    (_, _, c), rows, quarter = where(), mine.shape[0], block_a.shape[1]
    first, second = pick(c, mine[...], theirs[...]), pick(c, theirs[...], mine[...])
    block_a[:rows], block_b[:rows] = first[:, :quarter], first[:, quarter:]
    block_a[rows:], block_b[rows:] = second[:, :quarter], second[:, quarter:]


def gather_2_kernel(block_a, block_b, block_z, above, below, up, down, along, pair):
    (_, z, _), tall = where(), block_a.shape[0]
    wide, mid = 2 * tall, tall // 2
    for out in (up, down, pair):
        out[:tall] = pick(z, block_b[...], block_z[...])
        out[tall:wide] = pick(z, block_z[...], block_b[...])
    up[wide:] = below[:mid]
    down[wide:] = above[mid:]
    along[0] = above[...]
    along[1] = below[...]
    along[2] = block_a[...]


def gather_3_kernel(got_up, got_down, line):
    tall = line.shape[0]
    wide, mid = 2 * tall, tall // 2
    line[:mid] = got_up[wide:]
    line[mid:] = got_down[wide:]


def project(mine, theirs, whole, total):
    count = mine.shape[0]
    total[:count] += dot(mine, whole)
    total[count:] += dot(theirs, whole)


def order_z(z, own, other, whole):
    tall, quarter = own.shape
    whole[:tall, :quarter] = pick(z, own, other)
    whole[tall:, :quarter] = pick(z, other, own)


def project_r_kernel(mine, theirs, along, got_z, own_up, got_up, got_down, total, whole):
    _, z, _ = where()
    wide, quarter = whole.shape[0], got_up.shape[1]
    total[...] = jnp.zeros_like(total)
    for k, part in enumerate((got_down, got_up, own_up)):
        order_z(z, along[k], got_z[k], whole)
        whole[:, quarter:] = part[:wide]
        project(mine[k], theirs[k], whole[...], total)


def project_2_kernel(mine, theirs, line, got_z, pair, before, own, other, whole, total):
    _, z, _ = where()
    tall, quarter = line.shape
    count = own.shape[0]
    order_z(z, line[...], got_z[...], whole)
    whole[:, quarter:] = pair[...]
    total[...] = before[...]
    project(mine[...], theirs[...], whole[...], total)
    own[...] = (total[:count] * D ** (-0.5)).astype(BF)
    other[...] = (total[count:] * D ** (-0.5)).astype(BF)


def place_kernel(own, other, values):
    (_, _, c), half = where(), own.shape[1]
    values[:, :half] = pick(c, own[...], other[...])
    values[:, half:] = pick(c, other[...], own[...])


def adam_kernel(rates, mine, other, master, first, second, new_first, new_second, updated, wire):
    (_, _, c), half = where(), mine.shape[1]

    def rows(i, carry):
        here = pl.ds(pl.multiple_of(i * 16, 16), 16)
        for j in range(2):
            there = slice(j * half, (j + 1) * half)
            grad = jnp.where(c == j, mine[here, :], other[here, :].astype(F32)) * D ** (-0.5)
            moment = 0.9 * first[0, here, there] + 0.1 * grad
            square = 0.999 * second[0, here, there] + 0.001 * grad * grad
            scaled = square * rates[1]
            root = scaled * lax.rsqrt(scaled) + 1e-08
            guess = pl.reciprocal(root, approx=True)
            change = moment * rates[0] * (guess * (2.0 - root * guess))
            old = master[0, here, there]
            result = old - 0.02 * (change + 0.1 * old)
            new_first[0, here, there] = moment
            new_second[0, here, there] = square
            updated[here, there] = result
            wire[here, there] = result.astype(BF)
        return carry

    lax.fori_loop(0, mine.shape[0] // 16, rows, 0, unroll=2)


def adam(step, mine, other, master, first, second):
    _, rows, cols = master.shape
    half, tile = cols // 2, rows // 3
    time = (step[0] + 1).astype(F32)
    rate_one = 1.0 - jnp.exp(time * jnp.log(F32(0.9)))
    rate_two = 1.0 - jnp.exp(time * jnp.log(F32(0.999)))
    rates = jnp.stack([1.0 / rate_one, 1.0 / rate_two])
    part = pl.BlockSpec((tile, half), lambda i: (i, 0))
    full = pl.BlockSpec((1, tile, cols), lambda i: (0, i, 0))
    flat = pl.BlockSpec((tile, cols), lambda i: (i, 0))
    scalar = pl.BlockSpec(memory_space=pltpu.SMEM)
    return pl.pallas_call(
        adam_kernel,
        grid=(3,),
        in_specs=[scalar, part, part, full, full, full],
        out_specs=[full, full, flat, flat],
        out_shape=[
            shape(F32, 1, rows, cols),
            shape(F32, 1, rows, cols),
            shape(F32, rows, cols),
            shape(BF, rows, cols),
        ],
        cost_estimate=pl.CostEstimate(flops=20 * rows * cols, bytes_accessed=30 * rows * cols, transcendentals=0),
    )(rates, mine, other, master, first, second)


def on_device(tokens, cotangent, weight, first_moment, second_moment, step):
    _, _, c = where()
    master = weight[0]
    rows, cols = master.shape
    half, quarter, tall = cols // 2, cols // 4, rows * C
    wide, mid = 2 * tall, tall // 2
    tokens_here = tokens.shape[0]

    cot_mine = lax.dynamic_slice_in_dim(cotangent, c * half, half, 1)
    cot_theirs = hop(lax.dynamic_slice_in_dim(cotangent, (1 - c) * half, half, 1), dc=1)
    norm_2, norm_r = normalise(tokens)
    far_2 = hop(norm_2, dc=1)

    block = shape(BF, tall, quarter)
    product = pltpu.VMEM((wide, half), BF)
    low, high, near_2, got_2 = kernel_call(
        term_2_kernel,
        (norm_2, far_2, cot_mine, cot_theirs),
        (block,) * 4,
        (product,),
        limit=12,
        flops=4 * tokens_here * wide * half,
    )
    (send_r,) = after((norm_r,), low)
    far_r = hop(send_r, dc=1)
    three = shape(BF, 3, tall, quarter)
    part_a, near_r, got_r = kernel_call(
        term_r_kernel,
        (norm_r, far_r, cot_mine, cot_theirs),
        (shape(BF, 3, wide, quarter), three, three),
        (product,),
        limit=20,
        flops=12 * tokens_here * wide * half,
    )

    theirs = lax.dynamic_slice_in_dim(master, (1 - c) * half, half, 1).astype(BF)
    mine = lax.dynamic_slice_in_dim(master, c * half, half, 1).astype(BF)
    (theirs,) = after((theirs,), low)
    theirs = hop(theirs, dc=1)
    block_a, block_b = kernel_call(gather_1_kernel, (mine, theirs), (block, block), limit=8)
    low = hop(low, dy=1)
    high = hop(high, dy=-1)
    got_2 = hop(got_2, dz=1)
    got_r = hop(got_r, dz=1)
    long = shape(BF, wide + mid, quarter)
    up, down = kernel_call(scatter_2_kernel, (part_a, low, high, near_2, got_2), (long, long))
    send_a, send_b = after((block_a, block_b), up, down)
    from_below = hop(up, dy=1)
    from_above = hop(down, dy=-1)
    above = hop(send_a, dy=-1)
    below = hop(send_a, dy=1)
    block_z = hop(send_b, dz=1)
    block_f = shape(F32, tall, quarter)
    up, down, far_a, near_a, sum_b = kernel_call(
        scatter_3_kernel,
        (part_a, near_r, from_below, from_above, got_r),
        (block, block, block, block_f, block_f),
        (pltpu.VMEM((wide, quarter), F32),),
    )
    last_below = hop(up, dy=1)
    last_above = hop(down, dy=-1)
    last_z = hop(far_a, dz=1)
    own, other = kernel_call(
        scatter_4_kernel,
        (near_a, last_z, sum_b, last_below, last_above),
        (shape(F32, rows, half), shape(BF, rows, half)),
        (pltpu.VMEM((tall, half), F32),),
        limit=12,
    )
    other = hop(other, dc=1)

    up, down, along, pair = kernel_call(
        gather_2_kernel, (block_a, block_b, block_z, above, below), (long, long, three, shape(BF, wide, quarter))
    )
    up, down, along = after((up, down, along), last_below, last_above, last_z)
    got_up = hop(up, dy=1)
    got_down = hop(down, dy=-1)
    got_z = hop(along, dz=1)
    new_first, new_second, updated, wire = adam(step, own, other, weight, first_moment, second_moment)
    (pair,) = after((pair,), other)
    pair = hop(pair, dy=2)
    levels = lax.axis_size("peer").bit_length() - 1
    partner = lax.switch(step[0] % levels, [partial(gossip, bit=which) for which in range(levels)], wire)
    got_up, got_down = after((got_up, got_down), partner)
    (line,) = kernel_call(gather_3_kernel, (got_up, got_down), (block,), limit=8)
    line_z = hop(line, dz=1)

    whole = pltpu.VMEM((wide, half), BF)
    (total,) = kernel_call(
        project_r_kernel,
        (norm_r, far_r, along, got_z, up, got_up, got_down),
        (shape(F32, 2 * tokens_here, half),),
        (whole,),
        limit=20,
        flops=12 * tokens_here * wide * half,
    )
    result = shape(BF, tokens_here, half)
    result_own, result_other = kernel_call(
        project_2_kernel,
        (norm_2, far_2, line, line_z, pair, total),
        (result, result),
        (whole, pltpu.VMEM((2 * tokens_here, half), F32)),
        limit=16,
        flops=4 * tokens_here * wide * half,
    )
    (values,) = kernel_call(
        place_kernel, (result_own, hop(result_other, dc=1)), (shape(BF, tokens_here, cols),), limit=8
    )

    averaged = 0.5 * (updated + partner.astype(F32))
    return (values, averaged[None], new_first, new_second)


def solution(mesh):
    return jax.shard_map(
        on_device,
        mesh=mesh,
        in_specs=(
            P(("peer", "fsdp"), None),
            P(("peer", "fsdp"), None),
            P("peer", "fsdp", None),
            P("peer", "fsdp", None),
            P("peer", "fsdp", None),
            P(),
        ),
        out_specs=(
            P(("peer", "fsdp"), None),
            P("peer", "fsdp", None),
            P("peer", "fsdp", None),
            P("peer", "fsdp", None),
        ),
        check_vma=False,
    )
```
